32 devices in a mesh: row: 4 (over y, x), feat: 8 (over z, core).
Axes of the slice: x: 2, y: 2, z: 4, core: 2. Of those that a mesh axis runs over, the one named last changes fastest.
Arguments:
- node_features: bfloat16 [1024, 32768], P('feat', 'row'), may hold values from -6 to 6
- adjacency: bfloat16 [512, 128, 128], P('row'), may hold values from -0.5 to 0.5
- tile_row: int32 [512], P('row'), may hold values from 0 to 63
- tile_col: int32 [512], P('row'), may hold values from 0 to 63
- tile_count: int32 [4, 4], P('row'), may hold values from 1 to 32, as said below
- weight: bfloat16 [1024, 1024], P('feat'), may hold values from -0.1875 to 0.1875
- out_bias: float32 [1024], replicated, may hold values from -3 to 3
Outputs:
- activated: bfloat16 [1024, 32768], P('feat', 'row')
The draws below stay inside these ranges and needn't reach their ends.
Inputs may be any that keep to these rules, and one draw needn't show every extreme that they name: tile_count[r, s] is at least 1; the entry with s equal to r is 32.
All inputs are finite; a program needn't handle non-finite values.
Results may differ from the reference program's by a relative error of at most 0.0095.
Values may be sent and summed in bfloat16 or wider, within the bound.
A program may use at most 128 MiB of HBM per device.

```python
import jax
import jax.numpy as jnp

F = 1024
TILE = 128
ROWS_DEV = 8192
SLOTS = 32
NODES = 32768
N_ROW = 4


def draw_tile_count(key, part):
    first_key, second_key = jax.random.split(key)
    first_draw = jax.random.randint(first_key, (N_ROW, N_ROW), 1, SLOTS + 1)
    second_draw = jax.random.randint(second_key, (N_ROW, N_ROW), 1, SLOTS + 1)
    lesser = jnp.minimum(first_draw, second_draw)
    index_list = jnp.arange(N_ROW)
    diagonal = index_list[:, None] == index_list[None, :]
    return jnp.where(diagonal, SLOTS, lesser).astype(jnp.int32)


def plant(values, own_key, least, largest):
    spot = [jax.random.randint(jax.random.fold_in(own_key, axis), (), 0, length) for axis, length in enumerate(values.shape)]
    longest = values.shape.index(max(values.shape))
    neighbour = spot[:longest] + [(spot[longest] + 1) % values.shape[longest]] + spot[longest + 1:]
    return values.at[tuple(spot)].set(least).at[tuple(neighbour)].set(largest)


def levels(own_key, shape, pieces, smallest, high):
    def one(axis_at, shards_of):
        steps = jax.random.uniform(jax.random.fold_in(jax.random.fold_in(own_key, 6), axis_at), (shards_of,), jnp.float32, smallest / len(pieces), high / len(pieces))
        return jnp.repeat(jnp.exp(steps), shape[axis_at] // shards_of).reshape((-1,) + (1,) * (len(shape) - axis_at - 1))

    level = one(*pieces[0])
    for cut in pieces[1:]:
        level = level * one(*cut)
    return level


def normal_values(stream_key, dims, width, bound, shards=(), held_as=jnp.bfloat16):
    gain = levels(stream_key, dims, shards, -0.22, 0.18) if shards else 1.0
    array = jax.random.normal(stream_key, dims, jnp.float32) * width * gain
    return jnp.minimum(jnp.maximum(array, -bound), bound).astype(held_as)


def setup_inputs(seed: int = 0) -> dict:
    key_list = jax.random.split(jax.random.key(seed), 8)
    return {
        "node_features": normal_values(key_list[0], (F, NODES), 1.0, 6.0, ((0, 8), (1, 4))),
        "adjacency": normal_values(key_list[1], (N_ROW * N_ROW * SLOTS, TILE, TILE), TILE ** -0.5, 0.5, ((0, 4),)),
        "tile_row": plant(jax.random.randint(key_list[2], (N_ROW * N_ROW * SLOTS,), 0, ROWS_DEV // TILE), jax.random.fold_in(key_list[2], 1), 0, (ROWS_DEV // TILE) - 1).astype(jnp.int32),
        "tile_col": plant(jax.random.randint(key_list[3], (N_ROW * N_ROW * SLOTS,), 0, ROWS_DEV // TILE), jax.random.fold_in(key_list[3], 1), 0, (ROWS_DEV // TILE) - 1).astype(jnp.int32),
        "tile_count": draw_tile_count(jax.random.fold_in(key_list[7], 71), 0),
        "weight": normal_values(key_list[5], (F, F), F ** -0.5, 0.1875, ((0, 8),)),
        "out_bias": normal_values(key_list[6], (F,), 0.5, 3.0, (), jnp.float32),
    }


def source_term(held_block, tiles_part, rows_part, cols_part, live_count, row_blocks):
    feat_width = held_block.shape[0]
    blocks = held_block.reshape(feat_width, row_blocks, TILE)
    picked = jnp.take(blocks, cols_part, axis=1).astype(jnp.float32)
    product = jnp.einsum("fsj,sji->fsi", picked, tiles_part.astype(jnp.float32))
    slot_ids = jnp.arange(rows_part.shape[0]).astype(jnp.int32)
    live_mask = slot_ids < live_count
    block_ids = jnp.arange(row_blocks).astype(jnp.int32)
    onehot = ((rows_part[:, None] == block_ids[None, :]) & live_mask[:, None]).astype(jnp.float32)
    return jnp.einsum("fsi,sr->fri", product, onehot)


def reference(node_features, adjacency, tile_row, tile_col, tile_count, weight, out_bias):
    row_blocks = ROWS_DEV // TILE
    columns_out = []
    for row_dev in range(N_ROW):
        running = jnp.zeros((F, row_blocks, TILE), jnp.float32)
        for src_dev in range(N_ROW):
            first_slot = (row_dev * N_ROW + src_dev) * SLOTS
            running = running + source_term(
                node_features[:, src_dev * ROWS_DEV:(src_dev + 1) * ROWS_DEV],
                adjacency[first_slot:first_slot + SLOTS],
                tile_row[first_slot:first_slot + SLOTS],
                tile_col[first_slot:first_slot + SLOTS],
                tile_count[row_dev, src_dev],
                row_blocks)
        aggregated = running.reshape(F, ROWS_DEV).astype(jnp.bfloat16)
        pre_act = jnp.dot(weight, aggregated, preferred_element_type=jnp.float32) + out_bias[:, None]
        columns_out.append(jax.nn.relu(pre_act).astype(jnp.bfloat16))
    return jnp.concatenate(columns_out, axis=1)
```

```python
import functools

import jax
import jax.numpy as jnp
from jax import lax
from jax.experimental import pallas as pl
from jax.experimental.pallas import tpu as pltpu
from jax.sharding import PartitionSpec as P

CHUNKS = 4
MESH = pl.DeviceIdType.MESH


def exchange_kernel(rows, chips, x_ref, w_ref, y_ref, x_all, w_half, y_mine,
                    a1_s, a1_r, co_s, co_r, a2_s, a2_r, ro_s, ro_r, own_x, own_y,
                    wz_s, wz_r, wr_s, wr_r, own_w):
    width = x_ref.shape[0]
    chunk = x_all.shape[2]
    per_chip = CHUNKS * chunk
    blocks = chunk // y_ref.shape[3]
    part = w_ref.shape[1] // rows
    r = lax.axis_index("row")
    f = lax.axis_index("feat")
    z, c = f // 2, f % 2
    zs = [lax.rem(z + j, chips) for j in range(chips)]
    rs = [lax.rem(r + j, rows) for j in range(rows)]

    def dev(rr, zz, cc):
        return {"row": rr, "feat": zz * 2 + cc}

    barrier = pltpu.get_barrier_semaphore()
    partners = [dev(r, zz, c) for zz in zs[1:]] + [dev(rr, z, c) for rr in rs[1:]] + [dev(r, z, 1 - c)]
    for p in partners:
        pl.semaphore_signal(barrier, inc=1, device_id=p, device_id_type=MESH)
    pl.semaphore_wait(barrier, len(partners))

    def remote(src, dst, s, v, to):
        return pltpu.make_async_remote_copy(src_ref=src, dst_ref=dst, send_sem=s, recv_sem=v,
                                            device_id=to, device_id_type=MESH)

    def cols(k, zz):
        return pl.ds(pl.multiple_of(zz * per_chip + k * chunk, 128), chunk)

    def x_slot(k, zz, cc):
        return x_all.at[k, pl.ds(pl.multiple_of((zz * 2 + cc) * width, width), width), :]

    def a1_send(k, j):
        return remote(x_ref.at[:, cols(k, zs[j])], x_slot(k, z, c), a1_s.at[k, j], a1_r.at[k, z], dev(r, zs[j], c))

    def a1_recv(k, j):
        return remote(x_slot(k, zs[j], c), x_slot(k, zs[j], c), a1_s.at[k, j], a1_r.at[k, zs[j]], dev(r, zs[j], c))

    def co_send(k, j):
        src = x_ref.at[:, cols(k, z)] if j == 0 else x_slot(k, zs[j], c)
        return remote(src, x_slot(k, zs[j], c), co_s.at[k, j], co_r.at[k, zs[j]], dev(r, z, 1 - c))

    def co_recv(k, j):
        there = x_slot(k, zs[j], 1 - c)
        return remote(there, there, co_s.at[k, j], co_r.at[k, zs[j]], dev(r, z, 1 - c))

    def x_own(k):
        return pltpu.make_async_copy(x_ref.at[:, cols(k, z)], x_slot(k, z, c), own_x.at[k])

    def y_slot(rr, k, zz):
        return y_ref.at[rr, pl.ds(zz * (blocks * CHUNKS) + k * blocks, blocks)]

    def a2_send(k, j):
        return remote(y_mine.at[k, zs[j]], y_slot(r, k, z), a2_s.at[k, j], a2_r.at[k, z], dev(r, zs[j], c))

    def a2_recv(k, j):
        there = y_slot(r, k, zs[j])
        return remote(there, there, a2_s.at[k, j], a2_r.at[k, zs[j]], dev(r, zs[j], c))

    def y_own(k):
        return pltpu.make_async_copy(y_mine.at[k, z], y_slot(r, k, z), own_y.at[k])

    def ro_send(k, j, i):
        src = y_mine.at[k, z] if j == 0 else y_slot(r, k, zs[j])
        return remote(src, y_slot(r, k, zs[j]), ro_s.at[k, j, i], ro_r.at[k, zs[j], r], dev(rs[i], z, c))

    def ro_recv(k, j, i):
        there = y_slot(rs[i], k, zs[j])
        return remote(there, there, ro_s.at[k, j, i], ro_r.at[k, zs[j], rs[i]], dev(rs[i], z, c))

    def w_slot(zz, rr):
        return w_half.at[pl.ds(pl.multiple_of(zz * width, width), width), pl.ds(pl.multiple_of(rr * part, 128), part)]

    def wz_send(j):
        return remote(w_ref.at[:, pl.ds(pl.multiple_of(r * part, 128), part)], w_slot(z, r),
                      wz_s.at[j], wz_r.at[z], dev(r, zs[j], c))

    def wz_recv(j):
        return remote(w_slot(zs[j], r), w_slot(zs[j], r), wz_s.at[j], wz_r.at[zs[j]], dev(r, zs[j], c))

    def wr_send(j, i):
        return remote(w_slot(zs[j], r), w_slot(zs[j], r), wr_s.at[j, i], wr_r.at[zs[j], r], dev(rs[i], z, c))

    def wr_recv(j, i):
        there = w_slot(zs[j], rs[i])
        return remote(there, there, wr_s.at[j, i], wr_r.at[zs[j], rs[i]], dev(rs[i], z, c))

    w_own = pltpu.make_async_copy(w_ref, w_half.at[pl.ds(pl.multiple_of(z * width, width), width), :], own_w)
    others = range(1, chips)

    def start_a1(k):
        for j in others:
            a1_send(k, j).start()
        co_send(k, 0).start()
        x_own(k).start()

    def share_rows(k):
        for j in others:
            a2_recv(k, j).wait_recv()
            for i in range(1, rows):
                ro_send(k, j, i).start()

    for j in others:
        wz_send(j).start()
    w_own.start()
    start_a1(0)
    start_a1(1)
    for j in others:
        wz_recv(j).wait_recv()
        for i in range(1, rows):
            wr_send(j, i).start()

    for k in range(CHUNKS):
        for j in others:
            a1_recv(k, j).wait_recv()
            co_send(k, j).start()
        x_own(k).wait()
        for j in range(chips):
            co_recv(k, j).wait_recv()
        if k == 0:
            w_own.wait()
            for j in others:
                for i in range(1, rows):
                    wr_recv(j, i).wait_recv()
        step = min(256, chunk)
        tile = y_ref.shape[3]
        for n in range(chunk // step):
            prod = jnp.dot(w_half[...], x_all[k, :, n * step:(n + 1) * step],
                           preferred_element_type=jnp.float32).astype(jnp.bfloat16)
            for zz in range(chips):
                for b in range(step // tile):
                    y_mine[k, zz, n * (step // tile) + b] = prod[zz * width:(zz + 1) * width,
                                                                 b * tile:(b + 1) * tile]
        for j in others:
            a2_send(k, j).start()
        y_own(k).start()
        for i in range(1, rows):
            ro_send(k, 0, i).start()
        if k + 2 < CHUNKS:
            start_a1(k + 2)
        if k >= 1:
            share_rows(k - 1)
    share_rows(CHUNKS - 1)

    for j in others:
        wz_send(j).wait_send()
        for i in range(1, rows):
            wr_send(j, i).wait_send()
    for k in range(CHUNKS):
        y_own(k).wait()
        for j in range(chips):
            co_send(k, j).wait_send()
            if j:
                a1_send(k, j).wait_send()
                a2_send(k, j).wait_send()
            for i in range(1, rows):
                ro_send(k, j, i).wait_send()
                ro_recv(k, j, i).wait_recv()


def sum_kernel(rows, slots, row_ref, col_ref, count_ref, y_hbm, adj_hbm, bias_ref, out_ref,
               y_buf, adj_buf, acc, sems):
    blocks, width, tile = acc.shape
    group = 4

    def y_copy(s):
        return pltpu.make_async_copy(y_hbm.at[s], y_buf.at[s], sems.at[s, 0])

    def adj_copy(s):
        return pltpu.make_async_copy(adj_hbm.at[pl.ds(s * slots, slots)], adj_buf.at[pl.ds(s * slots, slots)],
                                     sems.at[s, 1])

    for s in range(rows):
        y_copy(s).start()
        adj_copy(s).start()
    acc[...] = jnp.broadcast_to(bias_ref[...][None], acc.shape)
    for s in range(rows):
        y_copy(s).wait()
        adj_copy(s).wait()
        live = count_ref[0, s]

        def body(g, carry):
            prods = []
            for u in range(group):
                t = s * slots + g * group + u
                prod = jnp.dot(y_buf[s, col_ref[t]], adj_buf[t], preferred_element_type=jnp.float32)
                prods.append(jnp.where(g * group + u < live, prod, 0.0))
            for u in range(group):
                at = row_ref[s * slots + g * group + u]
                acc[at] = acc[at] + prods[u]
            return carry

        lax.fori_loop(0, (live + group - 1) // group, body, 0)
    for b in range(blocks):
        out_ref[:, b * tile:(b + 1) * tile] = jnp.maximum(acc[b], 0.0).astype(jnp.bfloat16)


def on_device(rows, feats, node_features, adjacency, tile_row, tile_col, tile_count, weight, out_bias):
    width, nodes = node_features.shape
    tile = adjacency.shape[1]
    chips = feats // 2
    chunk = nodes // chips // CHUNKS
    slots = tile_row.shape[0] // rows
    dma = pltpu.SemaphoreType.DMA
    anywhere = pl.BlockSpec(memory_space=pl.ANY)
    y_all = pl.pallas_call(
        functools.partial(exchange_kernel, rows, chips),
        out_shape=jax.ShapeDtypeStruct((rows, nodes // tile, width, tile), jnp.bfloat16),
        in_specs=[anywhere] * 2,
        out_specs=anywhere,
        scratch_shapes=[
            pltpu.VMEM((CHUNKS, feats * width, chunk), jnp.bfloat16),
            pltpu.VMEM((chips * width, weight.shape[1]), jnp.bfloat16),
            pltpu.VMEM((CHUNKS, chips, chunk // tile, width, tile), jnp.bfloat16),
            dma((CHUNKS, chips)), dma((CHUNKS, chips)), dma((CHUNKS, chips)), dma((CHUNKS, chips)),
            dma((CHUNKS, chips)), dma((CHUNKS, chips)),
            dma((CHUNKS, chips, rows)), dma((CHUNKS, chips, rows)),
            dma((CHUNKS,)), dma((CHUNKS,)),
            dma((chips,)), dma((chips,)), dma((chips, rows)), dma((chips, rows)), dma(()),
        ],
        compiler_params=pltpu.CompilerParams(collective_id=0, has_side_effects=True,
                                             vmem_limit_bytes=24 << 20),
        cost_estimate=pl.CostEstimate(flops=2 * (feats * width) * width * nodes, bytes_accessed=24 << 20,
                                      transcendentals=0),
    )(node_features, weight)
    bias_here = lax.dynamic_slice_in_dim(out_bias, lax.axis_index("feat") * width, width, 0)
    smem = pl.BlockSpec(memory_space=pltpu.SMEM)
    vmem = pl.BlockSpec(memory_space=pltpu.VMEM)
    return pl.pallas_call(
        functools.partial(sum_kernel, rows, slots),
        out_shape=jax.ShapeDtypeStruct((width, nodes), jnp.bfloat16),
        in_specs=[smem, smem, smem, anywhere, anywhere, vmem],
        out_specs=vmem,
        scratch_shapes=[
            pltpu.VMEM(y_all.shape, jnp.bfloat16),
            pltpu.VMEM(adjacency.shape, jnp.bfloat16),
            pltpu.VMEM((nodes // tile, width, tile), jnp.float32),
            dma((rows, 2)),
        ],
        compiler_params=pltpu.CompilerParams(vmem_limit_bytes=40 << 20),
    )(tile_row, tile_col, tile_count, y_all, adjacency, jnp.broadcast_to(bias_here[:, None], (width, tile)))


def solution(mesh):
    in_specs = (
        P("feat", "row"),
        P("row", None, None),
        P("row"),
        P("row"),
        P("row", None),
        P("feat", None),
        P(),
    )
    out_specs = P("feat", "row")
    return jax.shard_map(
        functools.partial(on_device, mesh.shape["row"], mesh.shape["feat"]),
        mesh=mesh, in_specs=in_specs, out_specs=out_specs, check_vma=False,
    )
```

```python
import functools

import jax
import jax.numpy as jnp
from jax import lax
from jax.experimental import pallas as pl
from jax.experimental.pallas import tpu as pltpu
from jax.sharding import PartitionSpec as P

BLOCKS = 2
AHEAD = 2
MESH = pl.DeviceIdType.MESH


def exchange_kernel(rows, chips, x_ref, w_ref, y_ref, x_all, w_half, y_mine,
                    a1_s, a1_r, co_s, co_r, a2_s, a2_r, ro_s, ro_r, own_x, own_y,
                    wz_s, wz_r, wr_s, wr_r, own_w):
    width = x_ref.shape[0]
    chunks, _, chunk = x_all.shape
    per_chip = chunks * chunk
    blocks = chunk // y_ref.shape[3]
    part = w_ref.shape[1] // rows
    r = lax.axis_index("row")
    f = lax.axis_index("feat")
    z, c = f // 2, f % 2
    zs = [lax.rem(z + j, chips) for j in range(chips)]
    rs = [lax.rem(r + j, rows) for j in range(rows)]

    def dev(rr, zz, cc):
        return {"row": rr, "feat": zz * 2 + cc}

    barrier = pltpu.get_barrier_semaphore()
    partners = [dev(r, zz, c) for zz in zs[1:]] + [dev(rr, z, c) for rr in rs[1:]] + [dev(r, z, 1 - c)]
    for p in partners:
        pl.semaphore_signal(barrier, inc=1, device_id=p, device_id_type=MESH)
    pl.semaphore_wait(barrier, len(partners))

    def remote(src, dst, s, v, to):
        return pltpu.make_async_remote_copy(src_ref=src, dst_ref=dst, send_sem=s, recv_sem=v,
                                            device_id=to, device_id_type=MESH)

    def cols(k, zz):
        return pl.ds(pl.multiple_of(zz * per_chip + k * chunk, 128), chunk)

    def x_slot(k, zz, cc):
        return x_all.at[k, pl.ds(pl.multiple_of((zz * 2 + cc) * width, width), width), :]

    def a1_send(k, j):
        return remote(x_ref.at[:, cols(k, zs[j])], x_slot(k, z, c), a1_s.at[k, j], a1_r.at[k, z], dev(r, zs[j], c))

    def a1_recv(k, j):
        return remote(x_slot(k, zs[j], c), x_slot(k, zs[j], c), a1_s.at[k, j], a1_r.at[k, zs[j]], dev(r, zs[j], c))

    def co_send(k, j):
        src = x_ref.at[:, cols(k, z)] if j == 0 else x_slot(k, zs[j], c)
        return remote(src, x_slot(k, zs[j], c), co_s.at[k, j], co_r.at[k, zs[j]], dev(r, z, 1 - c))

    def co_recv(k, j):
        there = x_slot(k, zs[j], 1 - c)
        return remote(there, there, co_s.at[k, j], co_r.at[k, zs[j]], dev(r, z, 1 - c))

    def x_own(k):
        return pltpu.make_async_copy(x_ref.at[:, cols(k, z)], x_slot(k, z, c), own_x.at[k])

    def y_slot(rr, k, zz):
        return y_ref.at[rr, pl.ds(zz * (blocks * chunks) + k * blocks, blocks)]

    def a2_send(k, j):
        return remote(y_mine.at[k, zs[j]], y_slot(r, k, z), a2_s.at[k, j], a2_r.at[k, z], dev(r, zs[j], c))

    def a2_recv(k, j):
        there = y_slot(r, k, zs[j])
        return remote(there, there, a2_s.at[k, j], a2_r.at[k, zs[j]], dev(r, zs[j], c))

    def y_own(k):
        return pltpu.make_async_copy(y_mine.at[k, z], y_slot(r, k, z), own_y.at[k])

    square = rows == 4
    if square:
        near = [r, r + 1 - 2 * lax.rem(r, 2), lax.rem(r + 2, 4)]
        opposite = lax.rem(r + 2, 4) + 1 - 2 * lax.rem(r, 2)
    else:
        near = rs

    def ro_send(k, j, i):
        src = y_mine.at[k, z] if j == 0 else y_slot(r, k, zs[j])
        return remote(src, y_slot(r, k, zs[j]), ro_s.at[k, j, i], ro_r.at[k, zs[j], r], dev(near[i], z, c))

    def ro_recv(k, j, origin):
        there = y_slot(origin, k, zs[j])
        return remote(there, there, ro_s.at[k, j, 1], ro_r.at[k, zs[j], origin], dev(near[1], z, c))

    def on_send(k, j):
        first = 1 + (k + j) % 2
        there = y_slot(near[first], k, zs[j])
        return remote(there, there, ro_s.at[k, j, 3], ro_r.at[k, zs[j], near[first]], dev(near[3 - first], z, c))

    def hand_on(k):
        if square:
            for j in range(chips):
                ro_recv(k, j, near[1 + (k + j) % 2]).wait_recv()
                on_send(k, j).start()

    def w_slot(zz, rr):
        return w_half.at[pl.ds(pl.multiple_of(zz * width, width), width), pl.ds(pl.multiple_of(rr * part, 128), part)]

    def wz_send(j):
        return remote(w_ref.at[:, pl.ds(pl.multiple_of(r * part, 128), part)], w_slot(z, r),
                      wz_s.at[j], wz_r.at[z], dev(r, zs[j], c))

    def wz_recv(j):
        return remote(w_slot(zs[j], r), w_slot(zs[j], r), wz_s.at[j], wz_r.at[zs[j]], dev(r, zs[j], c))

    def wr_send(j, i):
        return remote(w_slot(zs[j], r), w_slot(zs[j], r), wr_s.at[j, i], wr_r.at[zs[j], r], dev(rs[i], z, c))

    def wr_recv(j, i):
        there = w_slot(zs[j], rs[i])
        return remote(there, there, wr_s.at[j, i], wr_r.at[zs[j], rs[i]], dev(rs[i], z, c))

    w_own = pltpu.make_async_copy(w_ref, w_half.at[pl.ds(pl.multiple_of(z * width, width), width), :], own_w)
    others = range(1, chips)

    def start_a1(k):
        for j in others:
            a1_send(k, j).start()
        co_send(k, 0).start()
        x_own(k).start()

    def share_rows(k):
        for j in others:
            a2_recv(k, j).wait_recv()
            for i in range(1, len(near)):
                ro_send(k, j, i).start()

    for j in others:
        wz_send(j).start()
    w_own.start()
    for k in range(AHEAD):
        start_a1(k)
    for j in others:
        wz_recv(j).wait_recv()
        for i in range(1, rows):
            wr_send(j, i).start()

    for k in range(chunks):
        for j in others:
            a1_recv(k, j).wait_recv()
            co_send(k, j).start()
        x_own(k).wait()
        for j in range(chips):
            co_recv(k, j).wait_recv()
        if k == 0:
            w_own.wait()
            for j in others:
                for i in range(1, rows):
                    wr_recv(j, i).wait_recv()
        step = min(256, chunk)
        tile = y_ref.shape[3]
        for n in range(chunk // step):
            prod = jnp.dot(w_half[...], x_all[k, :, n * step:(n + 1) * step],
                           preferred_element_type=jnp.float32).astype(jnp.bfloat16)
            for zz in range(chips):
                for b in range(step // tile):
                    y_mine[k, zz, n * (step // tile) + b] = prod[zz * width:(zz + 1) * width,
                                                                 b * tile:(b + 1) * tile]
        for j in others:
            a2_send(k, j).start()
        y_own(k).start()
        for i in range(1, len(near)):
            ro_send(k, 0, i).start()
        if k + AHEAD < chunks:
            start_a1(k + AHEAD)
        if k >= 1:
            share_rows(k - 1)
        if k >= 2:
            hand_on(k - 2)
    hand_on(chunks - 2)
    share_rows(chunks - 1)
    hand_on(chunks - 1)

    for j in others:
        wz_send(j).wait_send()
        for i in range(1, rows):
            wr_send(j, i).wait_send()
    for k in range(chunks):
        y_own(k).wait()
        for j in range(chips):
            co_send(k, j).wait_send()
            if j:
                a1_send(k, j).wait_send()
                a2_send(k, j).wait_send()
            for i in range(1, len(near)):
                ro_send(k, j, i).wait_send()
            if square:
                on_send(k, j).wait_send()
                ro_recv(k, j, near[2 - (k + j) % 2]).wait_recv()
                ro_recv(k, j, opposite).wait_recv()
            else:
                for i in range(1, rows):
                    ro_recv(k, j, near[i]).wait_recv()


def sum_kernel(rows, slots, row_ref, col_ref, count_ref, y_ref, adj_ref, bias_ref, out_ref, acc):
    blocks, width, tile = acc.shape
    group = 4
    acc[...] = jnp.broadcast_to(bias_ref[...][None], acc.shape)
    for s in range(rows):
        live = count_ref[0, s]

        def body(g, carry):
            prods = []
            for u in range(group):
                t = s * slots + g * group + u
                prod = jnp.dot(y_ref[s, col_ref[t]], adj_ref[t], preferred_element_type=jnp.float32)
                prods.append(jnp.where(g * group + u < live, prod, 0.0))
            for u in range(group):
                at = row_ref[s * slots + g * group + u]
                acc[at] = acc[at] + prods[u]
            return carry

        lax.fori_loop(0, (live + group - 1) // group, body, 0)
    for b in range(blocks):
        out_ref[:, b * tile:(b + 1) * tile] = jnp.maximum(acc[b], 0.0).astype(jnp.bfloat16)


def on_device(rows, feats, node_features, adjacency, tile_row, tile_col, tile_count, weight, out_bias):
    width, nodes = node_features.shape
    tile = adjacency.shape[1]
    chips = feats // 2
    chunk = BLOCKS * tile
    chunks = nodes // chips // chunk
    slots = tile_row.shape[0] // rows
    dma = pltpu.SemaphoreType.DMA
    anywhere = pl.BlockSpec(memory_space=pl.ANY)
    y_all = pl.pallas_call(
        functools.partial(exchange_kernel, rows, chips),
        out_shape=jax.ShapeDtypeStruct((rows, nodes // tile, width, tile), jnp.bfloat16),
        in_specs=[anywhere] * 2,
        out_specs=anywhere,
        scratch_shapes=[
            pltpu.VMEM((chunks, feats * width, chunk), jnp.bfloat16),
            pltpu.VMEM((chips * width, weight.shape[1]), jnp.bfloat16),
            pltpu.VMEM((chunks, chips, chunk // tile, width, tile), jnp.bfloat16),
            dma((chunks, chips)), dma((chunks, chips)), dma((chunks, chips)), dma((chunks, chips)),
            dma((chunks, chips)), dma((chunks, chips)),
            dma((chunks, chips, rows)), dma((chunks, chips, rows)),
            dma((chunks,)), dma((chunks,)),
            dma((chips,)), dma((chips,)), dma((chips, rows)), dma((chips, rows)), dma(()),
        ],
        compiler_params=pltpu.CompilerParams(collective_id=0, has_side_effects=True,
                                             vmem_limit_bytes=24 << 20),
        cost_estimate=pl.CostEstimate(flops=2 * (feats * width) * width * nodes, bytes_accessed=24 << 20,
                                      transcendentals=0),
    )(node_features, weight)
    bias_here = lax.dynamic_slice_in_dim(out_bias, lax.axis_index("feat") * width, width, 0)
    smem = pl.BlockSpec(memory_space=pltpu.SMEM)
    vmem = pl.BlockSpec(memory_space=pltpu.VMEM)
    return pl.pallas_call(
        functools.partial(sum_kernel, rows, slots),
        out_shape=jax.ShapeDtypeStruct((width, nodes), jnp.bfloat16),
        in_specs=[smem, smem, smem, vmem, vmem, vmem],
        out_specs=vmem,
        scratch_shapes=[
            pltpu.VMEM((nodes // tile, width, tile), jnp.float32),
        ],
        compiler_params=pltpu.CompilerParams(vmem_limit_bytes=40 << 20),
    )(tile_row, tile_col, tile_count, y_all, adjacency, jnp.broadcast_to(bias_here[:, None], (width, tile)))


def solution(mesh):
    in_specs = (
        P("feat", "row"),
        P("row", None, None),
        P("row"),
        P("row"),
        P("row", None),
        P("feat", None),
        P(),
    )
    out_specs = P("feat", "row")
    return jax.shard_map(
        functools.partial(on_device, mesh.shape["row"], mesh.shape["feat"]),
        mesh=mesh, in_specs=in_specs, out_specs=out_specs, check_vma=False,
    )
```

```python
import functools

import jax
import jax.numpy as jnp
from jax import lax
from jax.experimental import pallas as pl
from jax.experimental.pallas import tpu as pltpu
from jax.sharding import PartitionSpec as P

BLOCKS = 2
AHEAD = 2
MESH = pl.DeviceIdType.MESH


def exchange_kernel(rows, chips, x_ref, w_ref, y_ref, x_all, w_half, y_mine,
                    a1_s, a1_r, co_s, co_r, a2_s, a2_r, ro_s, ro_r, own_x, own_y,
                    wz_s, wz_r, wr_s, wr_r, own_w):
    width = x_ref.shape[0]
    chunks, _, chunk = x_all.shape
    per_chip = chunks * chunk
    blocks = chunk // y_ref.shape[3]
    part = w_ref.shape[1] // rows
    r = lax.axis_index("row")
    f = lax.axis_index("feat")
    z, c = f // 2, f % 2
    zs = [lax.rem(z + j, chips) for j in range(chips)]
    rs = [lax.rem(r + j, rows) for j in range(rows)]

    def dev(rr, zz, cc):
        return {"row": rr, "feat": zz * 2 + cc}

    barrier = pltpu.get_barrier_semaphore()
    partners = [dev(r, zz, c) for zz in zs[1:]] + [dev(rr, z, c) for rr in rs[1:]] + [dev(r, z, 1 - c)]
    for p in partners:
        pl.semaphore_signal(barrier, inc=1, device_id=p, device_id_type=MESH)
    pl.semaphore_wait(barrier, len(partners))

    def remote(src, dst, s, v, to):
        return pltpu.make_async_remote_copy(src_ref=src, dst_ref=dst, send_sem=s, recv_sem=v,
                                            device_id=to, device_id_type=MESH)

    def cols(k, zz):
        return pl.ds(pl.multiple_of(zz * per_chip + k * chunk, 128), chunk)

    def x_slot(k, zz, cc):
        return x_all.at[k, pl.ds(pl.multiple_of((zz * 2 + cc) * width, width), width), :]

    def a1_send(k, j):
        return remote(x_ref.at[:, cols(k, zs[j])], x_slot(k, z, c), a1_s.at[k, j], a1_r.at[k, z], dev(r, zs[j], c))

    def a1_recv(k, j):
        return remote(x_slot(k, zs[j], c), x_slot(k, zs[j], c), a1_s.at[k, j], a1_r.at[k, zs[j]], dev(r, zs[j], c))

    def co_send(k, j):
        src = x_ref.at[:, cols(k, z)] if j == 0 else x_slot(k, zs[j], c)
        return remote(src, x_slot(k, zs[j], c), co_s.at[k, j], co_r.at[k, zs[j]], dev(r, z, 1 - c))

    def co_recv(k, j):
        there = x_slot(k, zs[j], 1 - c)
        return remote(there, there, co_s.at[k, j], co_r.at[k, zs[j]], dev(r, z, 1 - c))

    def x_own(k):
        return pltpu.make_async_copy(x_ref.at[:, cols(k, z)], x_slot(k, z, c), own_x.at[k])

    def y_slot(rr, k, zz):
        return y_ref.at[rr, pl.ds(zz * (blocks * chunks) + k * blocks, blocks)]

    def a2_send(k, j):
        return remote(y_mine.at[k, zs[j]], y_slot(r, k, z), a2_s.at[k, j], a2_r.at[k, z], dev(r, zs[j], c))

    def a2_recv(k, j):
        there = y_slot(r, k, zs[j])
        return remote(there, there, a2_s.at[k, j], a2_r.at[k, zs[j]], dev(r, zs[j], c))

    def y_own(k):
        return pltpu.make_async_copy(y_mine.at[k, z], y_slot(r, k, z), own_y.at[k])

    square = rows == 4
    if square:
        near = [r, r + 1 - 2 * lax.rem(r, 2), lax.rem(r + 2, 4)]
        opposite = lax.rem(r + 2, 4) + 1 - 2 * lax.rem(r, 2)
    else:
        near = rs

    def ro_send(k, j, i):
        src = y_mine.at[k, z] if j == 0 else y_slot(r, k, zs[j])
        return remote(src, y_slot(r, k, zs[j]), ro_s.at[k, j, i], ro_r.at[k, zs[j], r], dev(near[i], z, c))

    def ro_recv(k, j, origin):
        there = y_slot(origin, k, zs[j])
        return remote(there, there, ro_s.at[k, j, 1], ro_r.at[k, zs[j], origin], dev(near[1], z, c))

    def on_send(k, j):
        first = 1 + (k + j) % 2
        there = y_slot(near[first], k, zs[j])
        return remote(there, there, ro_s.at[k, j, 3], ro_r.at[k, zs[j], near[first]], dev(near[3 - first], z, c))

    def hand_on(k):
        if square:
            for j in range(chips):
                ro_recv(k, j, near[1 + (k + j) % 2]).wait_recv()
                on_send(k, j).start()

    def w_slot(zz, rr):
        return w_half.at[pl.ds(pl.multiple_of(zz * width, width), width), pl.ds(pl.multiple_of(rr * part, 128), part)]

    def wz_send(j):
        return remote(w_ref.at[:, pl.ds(pl.multiple_of(r * part, 128), part)], w_slot(z, r),
                      wz_s.at[j], wz_r.at[z], dev(r, zs[j], c))

    def wz_recv(j):
        return remote(w_slot(zs[j], r), w_slot(zs[j], r), wz_s.at[j], wz_r.at[zs[j]], dev(r, zs[j], c))

    def wr_send(j, i):
        return remote(w_slot(zs[j], r), w_slot(zs[j], r), wr_s.at[j, i], wr_r.at[zs[j], r], dev(rs[i], z, c))

    def wr_recv(j, i):
        there = w_slot(zs[j], rs[i])
        return remote(there, there, wr_s.at[j, i], wr_r.at[zs[j], rs[i]], dev(rs[i], z, c))

    w_own = pltpu.make_async_copy(w_ref, w_half.at[pl.ds(pl.multiple_of(z * width, width), width), :], own_w)
    others = range(1, chips)

    def start_a1(k):
        for j in others:
            a1_send(k, j).start()
        co_send(k, 0).start()
        x_own(k).start()

    def share_rows(k):
        for j in others:
            a2_recv(k, j).wait_recv()
            for i in range(1, len(near)):
                ro_send(k, j, i).start()

    for j in others:
        wz_send(j).start()
    w_own.start()
    for k in range(AHEAD):
        start_a1(k)
    for j in others:
        wz_recv(j).wait_recv()
        for i in range(1, rows):
            wr_send(j, i).start()

    for k in range(chunks):
        for j in others:
            a1_recv(k, j).wait_recv()
            co_send(k, j).start()
        x_own(k).wait()
        for j in range(chips):
            co_recv(k, j).wait_recv()
        if k == 0:
            w_own.wait()
            for j in others:
                for i in range(1, rows):
                    wr_recv(j, i).wait_recv()
        step = min(256, chunk)
        tile = y_ref.shape[3]
        for n in range(chunk // step):
            prod = jnp.dot(w_half[...], x_all[k, :, n * step:(n + 1) * step],
                           preferred_element_type=jnp.float32).astype(jnp.bfloat16)
            for zz in range(chips):
                for b in range(step // tile):
                    y_mine[k, zz, n * (step // tile) + b] = prod[zz * width:(zz + 1) * width,
                                                                 b * tile:(b + 1) * tile]
        for j in others:
            a2_send(k, j).start()
        y_own(k).start()
        for i in range(1, len(near)):
            ro_send(k, 0, i).start()
        if k + AHEAD < chunks:
            start_a1(k + AHEAD)
        if k >= 1:
            share_rows(k - 1)
        if k >= 2:
            hand_on(k - 2)
    hand_on(chunks - 2)
    share_rows(chunks - 1)
    hand_on(chunks - 1)

    for j in others:
        wz_send(j).wait_send()
        for i in range(1, rows):
            wr_send(j, i).wait_send()
    for k in range(chunks):
        y_own(k).wait()
        for j in range(chips):
            co_send(k, j).wait_send()
            if j:
                a1_send(k, j).wait_send()
                a2_send(k, j).wait_send()
            for i in range(1, len(near)):
                ro_send(k, j, i).wait_send()
            if square:
                on_send(k, j).wait_send()
                ro_recv(k, j, near[2 - (k + j) % 2]).wait_recv()
                ro_recv(k, j, opposite).wait_recv()
            else:
                for i in range(1, rows):
                    ro_recv(k, j, near[i]).wait_recv()


def sum_kernel(rows, slots, row_ref, col_ref, count_ref, y_ref, adj_ref, bias_ref, out_ref, acc):
    blocks, width, tile = acc.shape
    group = 4
    acc[...] = jnp.broadcast_to(bias_ref[...][None], acc.shape)
    for s in range(rows):
        live = count_ref[0, s]

        def body(g, carry):
            prods = []
            for u in range(group):
                t = s * slots + g * group + u
                prod = jnp.dot(y_ref[s, col_ref[t]], adj_ref[t], preferred_element_type=jnp.float32)
                prods.append(jnp.where(g * group + u < live, prod, 0.0))
            for u in range(group):
                at = row_ref[s * slots + g * group + u]
                acc[at] = acc[at] + prods[u]
            return carry

        lax.fori_loop(0, (live + group - 1) // group, body, 0)
    for b in range(blocks):
        out_ref[:, b * tile:(b + 1) * tile] = jnp.maximum(acc[b], 0.0).astype(jnp.bfloat16)


def lists_kernel(rows, mine_ref, all_ref, send, recv, own):
    r = lax.axis_index("row")
    f = lax.axis_index("feat")
    rs = [lax.rem(r + j, rows) for j in range(rows)]
    barrier = pltpu.get_barrier_semaphore()
    for rr in rs[1:]:
        pl.semaphore_signal(barrier, inc=1, device_id={"row": rr, "feat": f}, device_id_type=MESH)
    pl.semaphore_wait(barrier, rows - 1)
    here = pltpu.make_async_copy(mine_ref, all_ref.at[r], own)
    here.start()
    sends = [pltpu.make_async_remote_copy(src_ref=mine_ref, dst_ref=all_ref.at[r], send_sem=send.at[j],
                                          recv_sem=recv.at[r], device_id={"row": rs[j], "feat": f},
                                          device_id_type=MESH) for j in range(1, rows)]
    for copy in sends:
        copy.start()
    for j in range(1, rows):
        there = all_ref.at[rs[j]]
        pltpu.make_async_remote_copy(src_ref=there, dst_ref=there, send_sem=send.at[j], recv_sem=recv.at[rs[j]],
                                     device_id={"row": rs[j], "feat": f}, device_id_type=MESH).wait_recv()
    for copy in sends:
        copy.wait_send()
    here.wait()


def pack_kernel(list_ref, x_ref, out_ref):
    tile = 128
    for p in range(x_ref.shape[1] // tile):
        out_ref[:, p * tile:(p + 1) * tile] = x_ref[:, pl.ds(pl.multiple_of(list_ref[p] * tile, tile), tile)]


def on_device(rows, feats, node_features, adjacency, tile_row, tile_col, tile_count, weight, out_bias):
    width, nodes = node_features.shape
    tile = adjacency.shape[1]
    chips = feats // 2
    slots = tile_row.shape[0] // rows
    blocks = nodes // tile
    dma = pltpu.SemaphoreType.DMA
    anywhere = pl.BlockSpec(memory_space=pl.ANY)
    smem = pl.BlockSpec(memory_space=pltpu.SMEM)
    vmem = pl.BlockSpec(memory_space=pltpu.VMEM)

    columns = tile_col.reshape(rows, slots)
    live = jnp.arange(slots)[None, :] < tile_count[0][:, None]
    high = -(-rows // 8) * 8
    mine = jnp.pad(jnp.where(live, columns, -1), ((0, high - rows), (0, 128 - slots)), constant_values=-1)
    lists = pl.pallas_call(
        functools.partial(lists_kernel, rows),
        out_shape=jax.ShapeDtypeStruct((rows, high, 128), jnp.int32),
        in_specs=[vmem], out_specs=vmem,
        scratch_shapes=[dma((rows,)), dma((rows,)), dma(())],
        compiler_params=pltpu.CompilerParams(collective_id=0, has_side_effects=True),
    )(mine)[:, :rows, :slots]
    ids = jnp.arange(blocks)
    used = jnp.any(lists[:, :, :, None] == ids, axis=(0, 2))
    most = jnp.max(jnp.sum(used.astype(jnp.int32), axis=1))
    places = jnp.sum((used[:, None, :] & (ids[None, None, :] < columns[:, :, None])).astype(jnp.int32), axis=2)
    places = jnp.where(live, places, 0).reshape(-1)
    used_here = lax.dynamic_index_in_dim(used, lax.axis_index("row"), 0, keepdims=False)
    rank = jnp.sum((used_here[None, :] & (ids[None, :] < ids[:, None])).astype(jnp.int32), axis=1)
    order = jnp.sum(jnp.where(used_here[None, :] & (rank[None, :] == ids[:, None]), ids[None, :], 0), axis=1)
    packed = pl.pallas_call(
        pack_kernel,
        out_shape=jax.ShapeDtypeStruct((width, nodes), jnp.bfloat16),
        in_specs=[smem, vmem], out_specs=vmem,
    )(order, node_features)
    bias_here = lax.dynamic_slice_in_dim(out_bias, lax.axis_index("feat") * width, width, 0)
    bias_tile = jnp.broadcast_to(bias_here[:, None], (width, tile))
    chunk = BLOCKS * tile

    def run(which, per_chip, packed, weight, row_ids, places, count, adjacency, bias_tile):
        chunks = per_chip // BLOCKS
        y_all = pl.pallas_call(
            functools.partial(exchange_kernel, rows, chips),
            out_shape=jax.ShapeDtypeStruct((rows, chips * per_chip, width, tile), jnp.bfloat16),
            in_specs=[anywhere] * 2,
            out_specs=anywhere,
            scratch_shapes=[
                pltpu.VMEM((chunks, feats * width, chunk), jnp.bfloat16),
                pltpu.VMEM((chips * width, weight.shape[1]), jnp.bfloat16),
                pltpu.VMEM((chunks, chips, chunk // tile, width, tile), jnp.bfloat16),
                dma((chunks, chips)), dma((chunks, chips)), dma((chunks, chips)), dma((chunks, chips)),
                dma((chunks, chips)), dma((chunks, chips)),
                dma((chunks, chips, rows)), dma((chunks, chips, rows)),
                dma((chunks,)), dma((chunks,)),
                dma((chips,)), dma((chips,)), dma((chips, rows)), dma((chips, rows)), dma(()),
            ],
            compiler_params=pltpu.CompilerParams(collective_id=1 + which, has_side_effects=True,
                                                 vmem_limit_bytes=24 << 20),
            cost_estimate=pl.CostEstimate(flops=2 * (feats * width) * width * nodes, bytes_accessed=24 << 20,
                                          transcendentals=0),
        )(packed, weight)
        return pl.pallas_call(
            functools.partial(sum_kernel, rows, slots),
            out_shape=jax.ShapeDtypeStruct((width, nodes), jnp.bfloat16),
            in_specs=[smem, smem, smem, vmem, vmem, vmem],
            out_specs=vmem,
            scratch_shapes=[pltpu.VMEM((blocks, width, tile), jnp.float32)],
            compiler_params=pltpu.CompilerParams(vmem_limit_bytes=40 << 20),
        )(row_ids, places, count, y_all, adjacency, bias_tile)

    full = blocks // chips
    sizes = sorted({max(2 * BLOCKS, full - BLOCKS * i) for i in range(3)})
    pick = sum((most > chips * size).astype(jnp.int32) for size in sizes[:-1])
    return lax.switch(pick, [functools.partial(run, i, size) for i, size in enumerate(sizes)],
                      packed, weight, tile_row, places, tile_count, adjacency, bias_tile)


def solution(mesh):
    in_specs = (
        P("feat", "row"),
        P("row", None, None),
        P("row"),
        P("row"),
        P("row", None),
        P("feat", None),
        P(),
    )
    out_specs = P("feat", "row")
    return jax.shard_map(
        functools.partial(on_device, mesh.shape["row"], mesh.shape["feat"]),
        mesh=mesh, in_specs=in_specs, out_specs=out_specs, check_vma=False,
    )
```

```python
import functools

import jax
import jax.numpy as jnp
from jax import lax
from jax.experimental import pallas as pl
from jax.experimental.pallas import tpu as pltpu
from jax.sharding import PartitionSpec as P

BLOCKS = 2
AHEAD = 1
MESH = pl.DeviceIdType.MESH


def exchange_kernel(rows, chips, x_ref, w_ref, y_ref, x_all, w_half, y_mine,
                    a1_s, a1_r, co_s, co_r, a2_s, a2_r, ro_s, ro_r, own_x, own_y,
                    wz_s, wz_r, wr_s, wr_r, own_w):
    width = x_ref.shape[0]
    chunks, _, chunk = x_all.shape
    per_chip = chunks * chunk
    blocks = chunk // y_ref.shape[3]
    part = w_ref.shape[1] // rows
    r = lax.axis_index("row")
    f = lax.axis_index("feat")
    z, c = f // 2, f % 2
    zs = [lax.rem(z + j, chips) for j in range(chips)]
    rs = [lax.rem(r + j, rows) for j in range(rows)]

    def dev(rr, zz, cc):
        return {"row": rr, "feat": zz * 2 + cc}

    barrier = pltpu.get_barrier_semaphore()
    partners = [dev(r, zz, c) for zz in zs[1:]] + [dev(rr, z, c) for rr in rs[1:]] + [dev(r, z, 1 - c)]
    for p in partners:
        pl.semaphore_signal(barrier, inc=1, device_id=p, device_id_type=MESH)
    pl.semaphore_wait(barrier, len(partners))

    def remote(src, dst, s, v, to):
        return pltpu.make_async_remote_copy(src_ref=src, dst_ref=dst, send_sem=s, recv_sem=v,
                                            device_id=to, device_id_type=MESH)

    def cols(k, zz):
        return pl.ds(pl.multiple_of(zz * per_chip + k * chunk, 128), chunk)

    def x_slot(k, zz, cc):
        return x_all.at[k, pl.ds(pl.multiple_of((zz * 2 + cc) * width, width), width), :]

    def a1_send(k, j):
        return remote(x_ref.at[:, cols(k, zs[j])], x_slot(k, z, c), a1_s.at[k, j], a1_r.at[k, z], dev(r, zs[j], c))

    def a1_recv(k, j):
        return remote(x_slot(k, zs[j], c), x_slot(k, zs[j], c), a1_s.at[k, j], a1_r.at[k, zs[j]], dev(r, zs[j], c))

    def co_send(k, j):
        src = x_ref.at[:, cols(k, z)] if j == 0 else x_slot(k, zs[j], c)
        return remote(src, x_slot(k, zs[j], c), co_s.at[k, j], co_r.at[k, zs[j]], dev(r, z, 1 - c))

    def co_recv(k, j):
        there = x_slot(k, zs[j], 1 - c)
        return remote(there, there, co_s.at[k, j], co_r.at[k, zs[j]], dev(r, z, 1 - c))

    def x_own(k):
        return pltpu.make_async_copy(x_ref.at[:, cols(k, z)], x_slot(k, z, c), own_x.at[k])

    def y_slot(rr, k, zz):
        return y_ref.at[rr, pl.ds(zz * (blocks * chunks) + k * blocks, blocks)]

    def a2_send(k, j):
        return remote(y_mine.at[k, zs[j]], y_slot(r, k, z), a2_s.at[k, j], a2_r.at[k, z], dev(r, zs[j], c))

    def a2_recv(k, j):
        there = y_slot(r, k, zs[j])
        return remote(there, there, a2_s.at[k, j], a2_r.at[k, zs[j]], dev(r, zs[j], c))

    def y_own(k):
        return pltpu.make_async_copy(y_mine.at[k, z], y_slot(r, k, z), own_y.at[k])

    square = rows == 4
    if square:
        near = [r, r + 1 - 2 * lax.rem(r, 2), lax.rem(r + 2, 4)]
        opposite = lax.rem(r + 2, 4) + 1 - 2 * lax.rem(r, 2)
    else:
        near = rs

    def ro_send(k, j, i):
        src = y_mine.at[k, z] if j == 0 else y_slot(r, k, zs[j])
        return remote(src, y_slot(r, k, zs[j]), ro_s.at[k, j, i], ro_r.at[k, zs[j], r], dev(near[i], z, c))

    def ro_recv(k, j, origin):
        there = y_slot(origin, k, zs[j])
        return remote(there, there, ro_s.at[k, j, 1], ro_r.at[k, zs[j], origin], dev(near[1], z, c))

    def on_send(k, j):
        first = 1 + (k + j) % 2
        there = y_slot(near[first], k, zs[j])
        return remote(there, there, ro_s.at[k, j, 3], ro_r.at[k, zs[j], near[first]], dev(near[3 - first], z, c))

    def hand_on(k):
        if square:
            for j in range(chips):
                ro_recv(k, j, near[1 + (k + j) % 2]).wait_recv()
                on_send(k, j).start()

    def w_slot(zz, rr):
        return w_half.at[pl.ds(pl.multiple_of(zz * width, width), width), pl.ds(pl.multiple_of(rr * part, 128), part)]

    def wz_send(j):
        return remote(w_ref.at[:, pl.ds(pl.multiple_of(r * part, 128), part)], w_slot(z, r),
                      wz_s.at[j], wz_r.at[z], dev(r, zs[j], c))

    def wz_recv(j):
        return remote(w_slot(zs[j], r), w_slot(zs[j], r), wz_s.at[j], wz_r.at[zs[j]], dev(r, zs[j], c))

    def wr_send(j, i):
        return remote(w_slot(zs[j], r), w_slot(zs[j], r), wr_s.at[j, i], wr_r.at[zs[j], r], dev(rs[i], z, c))

    def wr_recv(j, i):
        there = w_slot(zs[j], rs[i])
        return remote(there, there, wr_s.at[j, i], wr_r.at[zs[j], rs[i]], dev(rs[i], z, c))

    w_own = pltpu.make_async_copy(w_ref, w_half.at[pl.ds(pl.multiple_of(z * width, width), width), :], own_w)
    others = range(1, chips)

    def start_a1(k):
        for j in others:
            a1_send(k, j).start()
        co_send(k, 0).start()
        x_own(k).start()

    def share_rows(k):
        for j in others:
            a2_recv(k, j).wait_recv()
            for i in range(1, len(near)):
                ro_send(k, j, i).start()

    for j in others:
        wz_send(j).start()
    w_own.start()
    for k in range(AHEAD):
        start_a1(k)
    for j in others:
        wz_recv(j).wait_recv()
        for i in range(1, rows):
            wr_send(j, i).start()

    for k in range(chunks):
        for j in others:
            a1_recv(k, j).wait_recv()
            co_send(k, j).start()
        x_own(k).wait()
        for j in range(chips):
            co_recv(k, j).wait_recv()
        if k == 0:
            w_own.wait()
            for j in others:
                for i in range(1, rows):
                    wr_recv(j, i).wait_recv()
        step = min(256, chunk)
        tile = y_ref.shape[3]
        for n in range(chunk // step):
            prod = jnp.dot(w_half[...], x_all[k, :, n * step:(n + 1) * step],
                           preferred_element_type=jnp.float32).astype(jnp.bfloat16)
            for zz in range(chips):
                for b in range(step // tile):
                    y_mine[k, zz, n * (step // tile) + b] = prod[zz * width:(zz + 1) * width,
                                                                 b * tile:(b + 1) * tile]
        for j in others:
            a2_send(k, j).start()
        y_own(k).start()
        for i in range(1, len(near)):
            ro_send(k, 0, i).start()
        if k + AHEAD < chunks:
            start_a1(k + AHEAD)
        if k >= 1:
            share_rows(k - 1)
        if k >= 2:
            hand_on(k - 2)
    hand_on(chunks - 2)
    share_rows(chunks - 1)
    hand_on(chunks - 1)

    for j in others:
        wz_send(j).wait_send()
        for i in range(1, rows):
            wr_send(j, i).wait_send()
    for k in range(chunks):
        y_own(k).wait()
        for j in range(chips):
            co_send(k, j).wait_send()
            if j:
                a1_send(k, j).wait_send()
                a2_send(k, j).wait_send()
            for i in range(1, len(near)):
                ro_send(k, j, i).wait_send()
            if square:
                on_send(k, j).wait_send()
                ro_recv(k, j, near[2 - (k + j) % 2]).wait_recv()
                ro_recv(k, j, opposite).wait_recv()
            else:
                for i in range(1, rows):
                    ro_recv(k, j, near[i]).wait_recv()


def sum_kernel(rows, slots, row_ref, col_ref, count_ref, y_ref, adj_ref, bias_ref, out_ref, acc):
    blocks, width, tile = acc.shape
    group = 4
    acc[...] = jnp.broadcast_to(bias_ref[...][None], acc.shape)
    for s in range(rows):
        live = count_ref[0, s]

        def body(g, carry):
            prods = []
            for u in range(group):
                t = s * slots + g * group + u
                prod = jnp.dot(y_ref[s, col_ref[t]], adj_ref[t], preferred_element_type=jnp.float32)
                prods.append(jnp.where(g * group + u < live, prod, 0.0))
            for u in range(group):
                at = row_ref[s * slots + g * group + u]
                acc[at] = acc[at] + prods[u]
            return carry

        lax.fori_loop(0, (live + group - 1) // group, body, 0)
    for b in range(blocks):
        out_ref[:, b * tile:(b + 1) * tile] = jnp.maximum(acc[b], 0.0).astype(jnp.bfloat16)


def lists_kernel(rows, mine_ref, all_ref, send, recv, own):
    r = lax.axis_index("row")
    f = lax.axis_index("feat")
    rs = [lax.rem(r + j, rows) for j in range(rows)]
    barrier = pltpu.get_barrier_semaphore()
    for rr in rs[1:]:
        pl.semaphore_signal(barrier, inc=1, device_id={"row": rr, "feat": f}, device_id_type=MESH)
    pl.semaphore_wait(barrier, rows - 1)
    here = pltpu.make_async_copy(mine_ref, all_ref.at[r], own)
    here.start()
    sends = [pltpu.make_async_remote_copy(src_ref=mine_ref, dst_ref=all_ref.at[r], send_sem=send.at[j],
                                          recv_sem=recv.at[r], device_id={"row": rs[j], "feat": f},
                                          device_id_type=MESH) for j in range(1, rows)]
    for copy in sends:
        copy.start()
    for j in range(1, rows):
        there = all_ref.at[rs[j]]
        pltpu.make_async_remote_copy(src_ref=there, dst_ref=there, send_sem=send.at[j], recv_sem=recv.at[rs[j]],
                                     device_id={"row": rs[j], "feat": f}, device_id_type=MESH).wait_recv()
    for copy in sends:
        copy.wait_send()
    here.wait()


def pack_kernel(list_ref, x_ref, out_ref):
    tile = 128
    for p in range(x_ref.shape[1] // tile):
        out_ref[:, p * tile:(p + 1) * tile] = x_ref[:, pl.ds(pl.multiple_of(list_ref[p] * tile, tile), tile)]


def on_device(rows, feats, node_features, adjacency, tile_row, tile_col, tile_count, weight, out_bias):
    width, nodes = node_features.shape
    tile = adjacency.shape[1]
    chips = feats // 2
    slots = tile_row.shape[0] // rows
    blocks = nodes // tile
    dma = pltpu.SemaphoreType.DMA
    anywhere = pl.BlockSpec(memory_space=pl.ANY)
    smem = pl.BlockSpec(memory_space=pltpu.SMEM)
    vmem = pl.BlockSpec(memory_space=pltpu.VMEM)

    columns = tile_col.reshape(rows, slots)
    live = jnp.arange(slots)[None, :] < tile_count[0][:, None]
    high = -(-rows // 8) * 8
    mine = jnp.pad(jnp.where(live, columns, -1), ((0, high - rows), (0, 128 - slots)), constant_values=-1)
    lists = pl.pallas_call(
        functools.partial(lists_kernel, rows),
        out_shape=jax.ShapeDtypeStruct((rows, high, 128), jnp.int32),
        in_specs=[vmem], out_specs=vmem,
        scratch_shapes=[dma((rows,)), dma((rows,)), dma(())],
        compiler_params=pltpu.CompilerParams(collective_id=0, has_side_effects=True),
    )(mine)[:, :rows, :slots]
    ids = jnp.arange(blocks)
    used = jnp.any(lists[:, :, :, None] == ids, axis=(0, 2))
    most = jnp.max(jnp.sum(used.astype(jnp.int32), axis=1))
    places = jnp.sum((used[:, None, :] & (ids[None, None, :] < columns[:, :, None])).astype(jnp.int32), axis=2)
    places = jnp.where(live, places, 0).reshape(-1)
    used_here = lax.dynamic_index_in_dim(used, lax.axis_index("row"), 0, keepdims=False)
    rank = jnp.sum((used_here[None, :] & (ids[None, :] < ids[:, None])).astype(jnp.int32), axis=1)
    order = jnp.sum(jnp.where(used_here[None, :] & (rank[None, :] == ids[:, None]), ids[None, :], 0), axis=1)
    packed = pl.pallas_call(
        pack_kernel,
        out_shape=jax.ShapeDtypeStruct((width, nodes), jnp.bfloat16),
        in_specs=[smem, vmem], out_specs=vmem,
    )(order, node_features)
    bias_here = lax.dynamic_slice_in_dim(out_bias, lax.axis_index("feat") * width, width, 0)
    bias_tile = jnp.broadcast_to(bias_here[:, None], (width, tile))
    chunk = BLOCKS * tile

    def run(which, per_chip, packed, weight, row_ids, places, count, adjacency, bias_tile):
        chunks = per_chip // BLOCKS
        y_all = pl.pallas_call(
            functools.partial(exchange_kernel, rows, chips),
            out_shape=jax.ShapeDtypeStruct((rows, chips * per_chip, width, tile), jnp.bfloat16),
            in_specs=[anywhere] * 2,
            out_specs=anywhere,
            scratch_shapes=[
                pltpu.VMEM((chunks, feats * width, chunk), jnp.bfloat16),
                pltpu.VMEM((chips * width, weight.shape[1]), jnp.bfloat16),
                pltpu.VMEM((chunks, chips, chunk // tile, width, tile), jnp.bfloat16),
                dma((chunks, chips)), dma((chunks, chips)), dma((chunks, chips)), dma((chunks, chips)),
                dma((chunks, chips)), dma((chunks, chips)),
                dma((chunks, chips, rows)), dma((chunks, chips, rows)),
                dma((chunks,)), dma((chunks,)),
                dma((chips,)), dma((chips,)), dma((chips, rows)), dma((chips, rows)), dma(()),
            ],
            compiler_params=pltpu.CompilerParams(collective_id=1 + which, has_side_effects=True,
                                                 vmem_limit_bytes=24 << 20),
            cost_estimate=pl.CostEstimate(flops=2 * (feats * width) * width * nodes, bytes_accessed=24 << 20,
                                          transcendentals=0),
        )(packed, weight)
        return pl.pallas_call(
            functools.partial(sum_kernel, rows, slots),
            out_shape=jax.ShapeDtypeStruct((width, nodes), jnp.bfloat16),
            in_specs=[smem, smem, smem, vmem, vmem, vmem],
            out_specs=vmem,
            scratch_shapes=[pltpu.VMEM((blocks, width, tile), jnp.float32)],
            compiler_params=pltpu.CompilerParams(vmem_limit_bytes=40 << 20),
        )(row_ids, places, count, y_all, adjacency, bias_tile)

    full = blocks // chips
    sizes = sorted({max(2 * BLOCKS, full - BLOCKS * i) for i in range(3)})
    pick = sum((most > chips * size).astype(jnp.int32) for size in sizes[:-1])
    return lax.switch(pick, [functools.partial(run, i, size) for i, size in enumerate(sizes)],
                      packed, weight, tile_row, places, tile_count, adjacency, bias_tile)


def solution(mesh):
    in_specs = (
        P("feat", "row"),
        P("row", None, None),
        P("row"),
        P("row"),
        P("row", None),
        P("feat", None),
        P(),
    )
    out_specs = P("feat", "row")
    return jax.shard_map(
        functools.partial(on_device, mesh.shape["row"], mesh.shape["feat"]),
        mesh=mesh, in_specs=in_specs, out_specs=out_specs, check_vma=False,
    )
```
